768 devices in a mesh: section: 12 (over z), mp: 8 (over y_hi, core), dp: 8 (over x, y_lo).
Axes of the slice: x: 4, y: 8 (y_hi: 4, y_lo: 2; y = y_hi * 2 + y_lo), z: 12, core: 2. Of those that a mesh axis runs over, the one named last changes fastest.
Arguments:
- context: bfloat16 [12, 1024, 6144], P('section', None, 'mp'), may hold values from -6 to 6
- out_weight: bfloat16 [12, 6144, 8, 8, 192], P('section', 'mp', None, 'dp'), may hold values from -0.078125 to 0.078125
- residual: bfloat16 [12, 1024, 12288], P('section', None, ('mp', 'dp')), may hold values from -6 to 6
- layer_norm_gain: float32 [12, 12288], P('section', 'mp'), may hold values from 0.25 to 1.75
- layer_norm_bias: float32 [12, 12288], P('section', 'mp'), may hold values from -3 to 3
- ln_cotangent: bfloat16 [12, 1024, 12288], P('section', 'dp', 'mp'), may hold values from -6 to 6
Outputs:
- layer_norm_output: bfloat16 [12, 1024, 12288], P('section', 'dp', 'mp')
- resid_grad: bfloat16 [12, 1024, 12288], P('section', 'dp', 'mp')
The draws below stay inside these ranges and needn't reach their ends.
All inputs are finite; a program needn't handle non-finite values.
Results may differ from the reference program's by a relative error of at most 0.0047.
Values may be sent and summed in bfloat16 or wider, within the bound.
No kernel may reach another device: no remote copies, remote signals or barrier semaphores. Data moves between devices by JAX's collectives and lax.ppermute only.
A program may use at most 64 MiB of HBM per device.

```python
import jax
import jax.numpy as jnp
from jax import lax

D = 12288
TOK = 1024
HD = 6144
DB = 192
SECTIONS = 12
N_MP = 8
N_DP = 8


def block_scale(stream_key, dims, split, least, top_value):
    def one(axis_at, shards_of):
        heights = jax.random.uniform(jax.random.fold_in(jax.random.fold_in(stream_key, 6), axis_at), (shards_of,), jnp.float32, least / len(split), top_value / len(split))
        return jnp.repeat(jnp.exp(heights), dims[axis_at] // shards_of).reshape((-1,) + (1,) * (len(dims) - axis_at - 1))

    gain = one(*split[0])
    for cut in split[1:]:
        gain = gain * one(*cut)
    return gain


def normal_values(rng, dims, spread, most, split=(), held_as=jnp.bfloat16):
    gain = block_scale(rng, dims, split, -0.22, 0.18) if split else 1.0
    entries = jax.random.normal(rng, dims, jnp.float32) * spread * gain
    return jnp.minimum(jnp.maximum(entries, -most), most).astype(held_as)


def setup_inputs(seed: int = 0) -> dict:
    key_of = jax.random.split(jax.random.key(seed), 7)
    context = normal_values(key_of[0], (SECTIONS, TOK, HD), 1.0, 6.0, ((0, 12), (2, 8)))
    out_weight = normal_values(key_of[1], (SECTIONS, HD, N_MP, N_DP, DB), HD ** -0.5, 0.078125, ((0, 12), (1, 8), (3, 8)))
    residual = normal_values(key_of[2], (SECTIONS, TOK, D), 1.0, 6.0, ((0, 12), (2, 64)))
    layer_norm_gain = jnp.clip(1.0 + 0.15 * jax.random.normal(key_of[3], (SECTIONS, D), jnp.float32), 0.25, 1.75)
    layer_norm_bias = normal_values(key_of[4], (SECTIONS, D), 0.5, 3.0, ((0, 12), (1, 8)), jnp.float32)
    ln_cotangent = normal_values(key_of[5], (SECTIONS, TOK, D), 1.0, 6.0, ((0, 12), (1, 8), (2, 8)))
    return {"context": context, "out_weight": out_weight, "residual": residual, "layer_norm_gain": layer_norm_gain, "layer_norm_bias": layer_norm_bias, "ln_cotangent": ln_cotangent}


epsilon = 1e-05

def reference(context, out_weight, residual, layer_norm_gain, layer_norm_bias, ln_cotangent):
    weights = out_weight.reshape(SECTIONS, HD, D)

    def project(items):
        part_ctx, part_w, part_res = items
        summed = jnp.dot(part_ctx, part_w, preferred_element_type=jnp.float32)
        return (part_res.astype(jnp.float32) + summed).astype(jnp.bfloat16)
    section_out = lax.map(project, (context, weights, residual))
    arrived = jnp.roll(section_out, 1, axis=0).astype(jnp.float32)
    average = lax.optimization_barrier(jnp.mean(arrived, axis=-1, keepdims=True))
    centered_input = arrived - average
    variance = lax.optimization_barrier(jnp.mean(centered_input * centered_input, axis=-1, keepdims=True))
    inverse_deviation = lax.rsqrt(variance + epsilon)
    normalized_input = centered_input * inverse_deviation
    layer_norm_output = (normalized_input * layer_norm_gain[:, None, :] + layer_norm_bias[:, None, :]).astype(jnp.bfloat16)
    gain_scaled = ln_cotangent.astype(jnp.float32) * layer_norm_gain[:, None, :]
    input_mean = lax.optimization_barrier(jnp.mean(gain_scaled, axis=-1, keepdims=True))
    squared_mean = lax.optimization_barrier(jnp.mean(gain_scaled * normalized_input, axis=-1, keepdims=True))
    incoming_gradient = (inverse_deviation * (gain_scaled - input_mean - normalized_input * squared_mean)).astype(jnp.bfloat16)
    resid_grad = jnp.roll(incoming_gradient, -1, axis=0)
    return (layer_norm_output, resid_grad)
```

```python
import jax
import jax.numpy as jnp
from jax import lax
from jax.experimental import pallas as pl
from jax.experimental.pallas import tpu as pltpu
from jax.sharding import PartitionSpec as P

D = 12288
EPS = 1e-05
F32 = jnp.float32
BF16 = jnp.bfloat16
TB = 128
STEP = 2
ORDER = (2, 1, 3, 0)


def swap_core(x):
    n = lax.axis_size("mp")
    return lax.ppermute(x, "mp", [(i, i ^ 1) for i in range(n)])


def swap_y(x, pair):
    n = lax.axis_size("mp")
    return lax.ppermute(x, "mp", [(i, i ^ (2 * pair)) for i in range(n)])


def along_section(x, by):
    n = lax.axis_size("section")
    return lax.ppermute(x, "section", [(i, (i + by) % n) for i in range(n)])


def dot_t(w, c):
    return lax.dot_general(w, c, (((1,), (1,)), ((), ())), preferred_element_type=F32)


def params(mib):
    return pltpu.CompilerParams(vmem_limit_bytes=mib * 1024 * 1024)


def vmem(n):
    return [pl.BlockSpec(memory_space=pltpu.VMEM)] * n


def cost(n, rows, depth, toks):
    return pl.CostEstimate(flops=2 * n * rows * depth * toks, bytes_accessed=2 * n * rows * (depth + 2 * toks) + 2 * toks * depth, transcendentals=0)


def far_product(me, weights, ctx):
    n_blocks, rows, depth = weights.shape
    toks = ctx.shape[0]
    n_parts = 4

    def body(me_ref, w_ref, c_ref, far_ref, ctx_ref, near_w_ref, own_w_ref, far_w, c_sem, w_sem, own_sem):
        me = me_ref[0]
        core = me & 1

        def block(k, c):
            return (((me >> 1) ^ ORDER[k]) << 1) + c

        def c_copy(i):
            part = pl.ds(i * (toks // n_parts), toks // n_parts)
            return pltpu.make_async_copy(c_ref.at[part], ctx_ref.at[part], c_sem.at[i])

        def w_copy(k):
            to = far_w if k == 0 else near_w_ref.at[pl.ds((k - 1) * rows, rows)]
            return pltpu.make_async_copy(w_ref.at[block(k, 1 - core)], to, w_sem.at[k])

        def own_copy(k):
            return pltpu.make_async_copy(w_ref.at[block(k, core)], own_w_ref.at[pl.ds(k * rows, rows)], own_sem.at[k])

        w_copy(0).start()
        for i in range(n_parts):
            c_copy(i).start()
        for k in range(1, 4):
            w_copy(k).start()
        for k in range(4):
            own_copy(k).start()
        w_copy(0).wait()
        for i in range(n_parts):
            c_copy(i).wait()
        for i in range(toks // (STEP * TB)):
            acc = dot_t(far_w[...], ctx_ref[pl.ds(i * STEP * TB, STEP * TB)])
            for b in range(STEP):
                far_ref[STEP * i + b] = acc[:, b * TB:(b + 1) * TB].astype(BF16)
        for k in range(1, 4):
            w_copy(k).wait()
        for k in range(4):
            own_copy(k).wait()

    return pl.pallas_call(
        body,
        in_specs=[pl.BlockSpec(memory_space=pltpu.SMEM), pl.BlockSpec(memory_space=pltpu.HBM), pl.BlockSpec(memory_space=pltpu.HBM)],
        out_specs=vmem(4),
        out_shape=(
            jax.ShapeDtypeStruct((toks // TB, rows, TB), BF16),
            jax.ShapeDtypeStruct((toks, depth), BF16),
            jax.ShapeDtypeStruct((3 * rows, depth), BF16),
            jax.ShapeDtypeStruct((4 * rows, depth), BF16),
        ),
        scratch_shapes=[pltpu.VMEM((rows, depth), BF16), pltpu.SemaphoreType.DMA((n_parts,)), pltpu.SemaphoreType.DMA((4,)), pltpu.SemaphoreType.DMA((4,))],
        compiler_params=params(16), cost_estimate=cost(1, rows, depth, toks), name="far_product",
    )(me, weights, ctx)


def near_product(weights, ctx):
    toks, depth = ctx.shape
    rows = weights.shape[0] // 3

    def body(w_ref, c_ref, o_ref):
        for i in range(toks // (STEP * TB)):
            acc = dot_t(w_ref[...], c_ref[pl.ds(i * STEP * TB, STEP * TB)])
            for b in range(STEP):
                for k in range(3):
                    o_ref[k, STEP * i + b] = acc[k * rows:(k + 1) * rows, b * TB:(b + 1) * TB].astype(BF16)

    return pl.pallas_call(
        body, in_specs=vmem(2), out_specs=vmem(1)[0], out_shape=jax.ShapeDtypeStruct((3, toks // TB, rows, TB), BF16),
        compiler_params=params(16), cost_estimate=cost(3, rows, depth, toks), name="near_product",
    )(weights, ctx)


def far_sum(weights, ctx, other):
    toks, depth = ctx.shape
    rows = weights.shape[0] // 4
    half = rows // 2

    def body(w_ref, c_ref, r_ref, top_ref, low_ref):
        for i in range(toks // (STEP * TB)):
            acc = dot_t(w_ref[:rows], c_ref[pl.ds(i * STEP * TB, STEP * TB)])
            for b in range(STEP):
                total = (acc[:, b * TB:(b + 1) * TB] + r_ref[STEP * i + b].astype(F32)).astype(BF16)
                top_ref[STEP * i + b] = total[:half]
                low_ref[STEP * i + b] = total[half:]

    shape = jax.ShapeDtypeStruct((toks // TB, half, TB), BF16)
    return pl.pallas_call(
        body, in_specs=vmem(3), out_specs=vmem(2), out_shape=(shape, shape),
        compiler_params=params(16), cost_estimate=cost(1, rows, depth, toks), name="far_sum",
    )(weights, ctx, other)


def near_sum(weights, ctx, other, residual, cot, gain):
    toks, depth = ctx.shape
    rows = weights.shape[0] // 4
    half = rows // 2
    width = cot.shape[1]

    def body(w_ref, c_ref, r_ref, res_ref, cot_ref, gain_ref, one_ref, three_ref, keep_one_ref, keep_three_ref, mine_ref, pack_ref):
        pack_ref[:TB] = cot_ref[...]
        g = gain_ref[...]
        hi = g.astype(BF16)
        g = g - hi.astype(F32)
        mid = g.astype(BF16)
        low = (g - mid.astype(F32)).astype(BF16)
        row = lax.broadcasted_iota(jnp.int32, (16, width), 0)
        parts = jnp.where(row == 0, hi.astype(F32), jnp.where(row == 1, mid.astype(F32), jnp.where(row == 2, low.astype(F32), 0.0)))
        pack_ref[TB:] = parts.astype(BF16)
        for i in range(toks // (STEP * TB)):
            acc = dot_t(w_ref[rows:], c_ref[pl.ds(i * STEP * TB, STEP * TB)])
            for b in range(STEP):
                t = STEP * i + b
                cut = slice(b * TB, (b + 1) * TB)
                one = acc[:rows, cut] + r_ref[0, t].astype(F32)
                one_ref[t] = one[:half].astype(BF16)
                keep_one_ref[t] = one[half:]
                three = acc[rows:2 * rows, cut] + r_ref[1, t].astype(F32)
                three_ref[t] = three[half:].astype(BF16)
                keep_three_ref[t] = three[:half]
                mine_ref[t] = acc[2 * rows:, cut] + r_ref[2, t].astype(F32) + res_ref[:, t * TB:(t + 1) * TB].astype(F32)

    part = lambda dtype: jax.ShapeDtypeStruct((toks // TB, half, TB), dtype)
    return pl.pallas_call(
        body, in_specs=vmem(6), out_specs=vmem(6),
        out_shape=(part(BF16), part(BF16), part(F32), part(F32), jax.ShapeDtypeStruct((toks // TB, rows, TB), F32), jax.ShapeDtypeStruct((TB + 16, width), BF16)),
        compiler_params=params(20), cost_estimate=cost(3, rows, depth, toks), name="near_sum",
    )(weights, ctx, other, residual, cot, gain)


def add_halves(mine, top, low, dtype, name):
    half = top.shape[1]

    def body(mine_ref, top_ref, low_ref, o_ref):
        o_ref[:, :half] = (mine_ref[:, :half] + top_ref[...].astype(F32)).astype(dtype)
        o_ref[:, half:] = (mine_ref[:, half:] + low_ref[...].astype(F32)).astype(dtype)

    return pl.pallas_call(
        body, in_specs=vmem(3), out_specs=vmem(1)[0], out_shape=jax.ShapeDtypeStruct(mine.shape, dtype), name=name, compiler_params=params(8),
        cost_estimate=pl.CostEstimate(flops=mine.size, bytes_accessed=9 * mine.size, transcendentals=0),
    )(mine, top, low)


def relay_sum(keep_one, keep_three, from_one, from_three):
    def body(keep_one_ref, keep_three_ref, from_one_ref, from_three_ref, one_ref, three_ref):
        one_ref[...] = (keep_one_ref[...] + from_three_ref[...].astype(F32)).astype(BF16)
        three_ref[...] = (keep_three_ref[...] + from_one_ref[...].astype(F32)).astype(BF16)

    shape = jax.ShapeDtypeStruct(keep_one.shape, BF16)
    return pl.pallas_call(
        body, in_specs=vmem(4), out_specs=vmem(2), out_shape=(shape, shape), name="relay_sum", compiler_params=params(8),
        cost_estimate=pl.CostEstimate(flops=2 * keep_one.size, bytes_accessed=16 * keep_one.size, transcendentals=0),
    )(keep_one, keep_three, from_one, from_three)


def over_mp(x):
    n = lax.axis_size("mp")
    return jnp.sum(lax.all_to_all(jnp.broadcast_to(x, (n, *x.shape)), "mp", split_axis=0, concat_axis=0, tiled=True), axis=0)


def local(context, out_weight, residual, gain, bias, cot):
    m = lax.axis_index("mp").astype(jnp.int32)
    weights = out_weight[0][:, :, 0, :].transpose(1, 2, 0)
    weights = pltpu.with_memory_space_constraint(weights, pltpu.HBM)
    ctx = pltpu.with_memory_space_constraint(context[0], pltpu.HBM)

    far_sent, ctx, near_weights, own_weights = far_product(m.reshape(1), weights, ctx)
    far_got = swap_core(far_sent)
    near_got = swap_core(near_product(near_weights, ctx))
    far_top, far_low = far_sum(own_weights, ctx, far_got)
    relay_one = swap_y(far_top, 1)
    relay_three = swap_y(far_low, 3)
    one, three, keep_one, keep_three, mine, pack = near_sum(own_weights, ctx, near_got, residual[0].T, cot[0], gain)
    direct_one = swap_y(one, 1)
    direct_three = swap_y(three, 3)
    on_one, on_three = relay_sum(keep_one, keep_three, relay_one, relay_three)
    sum_one = swap_y(on_one, 1)
    sum_three = swap_y(on_three, 3)
    pack_next = along_section(pack, -1)
    mine = add_halves(mine, direct_one, direct_three, F32, "add_direct")
    section_out = add_halves(mine, sum_three, sum_one, BF16, "add_last")
    got = lax.all_to_all(section_out, "dp", split_axis=0, concat_axis=0, tiled=True)

    parts = pack_next[TB:TB + 3].astype(F32)
    gain_next = parts[0:1] + parts[1:2] + parts[2:3]
    scaled = pack_next[:TB].astype(F32) * gain_next
    width = float(D)

    got_next = along_section(got, 1)
    x = got.reshape(-1, TB).T.astype(F32)
    sums = jnp.stack([jnp.sum(x, -1), jnp.sum(x * x, -1), jnp.sum(scaled, -1), jnp.sum(scaled * x, -1)])
    sums = over_mp(sums)
    average = sums[0] / width
    rstd = lax.rsqrt(sums[1] / width - average * average + EPS)
    first = sums[2] / width
    second = rstd * (sums[3] / width - average * first)
    ar_next = along_section(jnp.stack([average, rstd]), 1)
    xhat = (x - average[:, None]) * rstd[:, None]
    grad = (rstd[:, None] * (scaled - first[:, None] - xhat * second[:, None])).astype(BF16)
    xn = got_next.reshape(-1, TB).T.astype(F32)
    out = ((xn - ar_next[0][:, None]) * ar_next[1][:, None] * gain + bias).astype(BF16)
    return out[None], grad[None]


def solution(mesh):
    in_specs = (
        P("section", None, "mp"),
        P("section", "mp", None, "dp", None),
        P("section", None, ("mp", "dp")),
        P("section", "mp"),
        P("section", "mp"),
        P("section", "dp", "mp"),
    )
    out_specs = (P("section", "dp", "mp"), P("section", "dp", "mp"))
    return jax.shard_map(local, mesh=mesh, in_specs=in_specs, out_specs=out_specs, check_vma=False)
```

```python
import jax
import jax.numpy as jnp
from jax import lax
from jax.experimental import pallas as pl
from jax.experimental.pallas import tpu as pltpu
from jax.sharding import PartitionSpec as P

D = 12288
EPS = 1e-05
F32 = jnp.float32
BF16 = jnp.bfloat16
TB = 128
STEP = 2
ORDER = (2, 1, 3, 0)


def swap_core(x):
    n = lax.axis_size("mp")
    return lax.ppermute(x, "mp", [(i, i ^ 1) for i in range(n)])


def swap_y(x, pair):
    n = lax.axis_size("mp")
    return lax.ppermute(x, "mp", [(i, i ^ (2 * pair)) for i in range(n)])


def along_section(x, by):
    n = lax.axis_size("section")
    return lax.ppermute(x, "section", [(i, (i + by) % n) for i in range(n)])


def dot_t(w, c):
    return lax.dot_general(w, c, (((1,), (1,)), ((), ())), preferred_element_type=F32)


def params(mib):
    return pltpu.CompilerParams(vmem_limit_bytes=mib * 1024 * 1024)


def vmem(n):
    return [pl.BlockSpec(memory_space=pltpu.VMEM)] * n


def cost(n, rows, depth, toks):
    return pl.CostEstimate(flops=2 * n * rows * depth * toks, bytes_accessed=2 * n * rows * (depth + 2 * toks) + 2 * toks * depth, transcendentals=0)


def far_product(me, weights, ctx):
    n_blocks, rows, depth = weights.shape
    toks = ctx.shape[0]
    n_parts = 4

    def body(me_ref, w_ref, c_ref, far_ref, ctx_ref, near_w_ref, own_w_ref, far_w, c_sem, w_sem, own_sem):
        me = me_ref[0]
        core = me & 1

        def block(k, c):
            return (((me >> 1) ^ ORDER[k]) << 1) + c

        def c_copy(i):
            part = pl.ds(i * (toks // n_parts), toks // n_parts)
            return pltpu.make_async_copy(c_ref.at[part], ctx_ref.at[part], c_sem.at[i])

        def w_copy(k):
            to = far_w if k == 0 else near_w_ref.at[pl.ds((k - 1) * rows, rows)]
            return pltpu.make_async_copy(w_ref.at[block(k, 1 - core)], to, w_sem.at[k])

        def own_copy(k):
            return pltpu.make_async_copy(w_ref.at[block(k, core)], own_w_ref.at[pl.ds(k * rows, rows)], own_sem.at[k])

        w_copy(0).start()
        for i in range(n_parts):
            c_copy(i).start()
        for k in range(1, 4):
            w_copy(k).start()
        for k in range(4):
            own_copy(k).start()
        w_copy(0).wait()
        for i in range(n_parts):
            c_copy(i).wait()
        for i in range(toks // (STEP * TB)):
            acc = dot_t(far_w[...], ctx_ref[pl.ds(i * STEP * TB, STEP * TB)])
            for b in range(STEP):
                far_ref[STEP * i + b] = acc[:, b * TB:(b + 1) * TB].astype(BF16)
        for k in range(1, 4):
            w_copy(k).wait()
        for k in range(4):
            own_copy(k).wait()

    return pl.pallas_call(
        body,
        in_specs=[pl.BlockSpec(memory_space=pltpu.SMEM), pl.BlockSpec(memory_space=pltpu.HBM), pl.BlockSpec(memory_space=pltpu.HBM)],
        out_specs=vmem(4),
        out_shape=(
            jax.ShapeDtypeStruct((toks // TB, rows, TB), BF16),
            jax.ShapeDtypeStruct((toks, depth), BF16),
            jax.ShapeDtypeStruct((3 * rows, depth), BF16),
            jax.ShapeDtypeStruct((4 * rows, depth), BF16),
        ),
        scratch_shapes=[pltpu.VMEM((rows, depth), BF16), pltpu.SemaphoreType.DMA((n_parts,)), pltpu.SemaphoreType.DMA((4,)), pltpu.SemaphoreType.DMA((4,))],
        compiler_params=params(16), cost_estimate=cost(1, rows, depth, toks), name="far_product",
    )(me, weights, ctx)


def near_product(weights, ctx, after):
    toks, depth = ctx.shape
    rows = weights.shape[0] // 3

    def body(w_ref, c_ref, after_ref, o_ref):
        for i in range(toks // (STEP * TB)):
            acc = dot_t(w_ref[...], c_ref[pl.ds(i * STEP * TB, STEP * TB)])
            for b in range(STEP):
                for k in range(3):
                    o_ref[k, STEP * i + b] = acc[k * rows:(k + 1) * rows, b * TB:(b + 1) * TB].astype(BF16)

    return pl.pallas_call(
        body, in_specs=[*vmem(2), pl.BlockSpec(memory_space=pl.ANY)], out_specs=vmem(1)[0], out_shape=jax.ShapeDtypeStruct((3, toks // TB, rows, TB), BF16),
        compiler_params=params(16), cost_estimate=cost(3, rows, depth, toks), name="near_product",
    )(weights, ctx, after)


def far_sum(weights, ctx, other):
    toks, depth = ctx.shape
    rows = weights.shape[0] // 4
    half = rows // 2

    def body(w_ref, c_ref, r_ref, top_ref, low_ref):
        for i in range(toks // (STEP * TB)):
            acc = dot_t(w_ref[:rows], c_ref[pl.ds(i * STEP * TB, STEP * TB)])
            for b in range(STEP):
                total = (acc[:, b * TB:(b + 1) * TB] + r_ref[STEP * i + b].astype(F32)).astype(BF16)
                top_ref[STEP * i + b] = total[:half]
                low_ref[STEP * i + b] = total[half:]

    shape = jax.ShapeDtypeStruct((toks // TB, half, TB), BF16)
    return pl.pallas_call(
        body, in_specs=vmem(3), out_specs=vmem(2), out_shape=(shape, shape),
        compiler_params=params(16), cost_estimate=cost(1, rows, depth, toks), name="far_sum",
    )(weights, ctx, other)


def near_sum(weights, ctx, other, residual):
    toks, depth = ctx.shape
    rows = weights.shape[0] // 4
    half = rows // 2

    def body(w_ref, c_ref, r_ref, res_ref, one_ref, three_ref, keep_one_ref, keep_three_ref, mine_ref):
        for i in range(toks // (STEP * TB)):
            acc = dot_t(w_ref[rows:], c_ref[pl.ds(i * STEP * TB, STEP * TB)])
            for b in range(STEP):
                t = STEP * i + b
                cut = slice(b * TB, (b + 1) * TB)
                one = acc[:rows, cut] + r_ref[0, t].astype(F32)
                one_ref[t] = one[:half].astype(BF16)
                keep_one_ref[t] = one[half:]
                three = acc[rows:2 * rows, cut] + r_ref[1, t].astype(F32)
                three_ref[t] = three[half:].astype(BF16)
                keep_three_ref[t] = three[:half]
                mine_ref[t] = acc[2 * rows:, cut] + r_ref[2, t].astype(F32) + res_ref[:, t * TB:(t + 1) * TB].astype(F32)

    part = lambda dtype: jax.ShapeDtypeStruct((toks // TB, half, TB), dtype)
    return pl.pallas_call(
        body, in_specs=vmem(4), out_specs=vmem(5),
        out_shape=(part(BF16), part(BF16), part(F32), part(F32), jax.ShapeDtypeStruct((toks // TB, rows, TB), F32)),
        compiler_params=params(20), cost_estimate=cost(3, rows, depth, toks), name="near_sum",
    )(weights, ctx, other, residual)


def add_direct(mine, top, low, cot, gain):
    half = top.shape[1]
    width = cot.shape[1]

    def body(mine_ref, top_ref, low_ref, cot_ref, gain_ref, o_ref, pack_ref):
        pack_ref[:TB] = cot_ref[...]
        g = gain_ref[...]
        hi = g.astype(BF16)
        g = g - hi.astype(F32)
        mid = g.astype(BF16)
        low = (g - mid.astype(F32)).astype(BF16)
        row = lax.broadcasted_iota(jnp.int32, (16, width), 0)
        parts = jnp.where(row == 0, hi.astype(F32), jnp.where(row == 1, mid.astype(F32), jnp.where(row == 2, low.astype(F32), 0.0)))
        pack_ref[TB:] = parts.astype(BF16)
        o_ref[:, :half] = mine_ref[:, :half] + top_ref[...].astype(F32)
        o_ref[:, half:] = mine_ref[:, half:] + low_ref[...].astype(F32)

    return pl.pallas_call(
        body, in_specs=vmem(5), out_specs=vmem(2), out_shape=(jax.ShapeDtypeStruct(mine.shape, F32), jax.ShapeDtypeStruct((TB + 16, width), BF16)),
        name="add_direct", compiler_params=params(8),
        cost_estimate=pl.CostEstimate(flops=1 * mine.size, bytes_accessed=9 * mine.size, transcendentals=0),
    )(mine, top, low, cot, gain)


def add_last(mine, top, low):
    half = top.shape[1]

    def body(mine_ref, top_ref, low_ref, o_ref):
        o_ref[:, :half] = (mine_ref[:, :half] + top_ref[...].astype(F32)).astype(BF16)
        o_ref[:, half:] = (mine_ref[:, half:] + low_ref[...].astype(F32)).astype(BF16)

    return pl.pallas_call(
        body, in_specs=vmem(3), out_specs=vmem(1)[0], out_shape=jax.ShapeDtypeStruct(mine.shape, BF16), name="add_last", compiler_params=params(8),
        cost_estimate=pl.CostEstimate(flops=20000 * mine.size, bytes_accessed=7 * mine.size, transcendentals=0),
    )(mine, top, low)


def relay_sum(keep_one, keep_three, from_one, from_three):
    def body(keep_one_ref, keep_three_ref, from_one_ref, from_three_ref, one_ref, three_ref):
        one_ref[...] = (keep_one_ref[...] + from_three_ref[...].astype(F32)).astype(BF16)
        three_ref[...] = (keep_three_ref[...] + from_one_ref[...].astype(F32)).astype(BF16)

    shape = jax.ShapeDtypeStruct(keep_one.shape, BF16)
    return pl.pallas_call(
        body, in_specs=vmem(4), out_specs=vmem(2), out_shape=(shape, shape), name="relay_sum", compiler_params=params(8),
        cost_estimate=pl.CostEstimate(flops=2 * keep_one.size, bytes_accessed=16 * keep_one.size, transcendentals=0),
    )(keep_one, keep_three, from_one, from_three)


def small(body, name, n_in, out_shape, *args, flops=0):
    n_out = len(out_shape) if isinstance(out_shape, tuple) else 1
    moved = sum(a.size * a.dtype.itemsize for a in args)
    return pl.pallas_call(
        body, in_specs=vmem(n_in), out_specs=vmem(n_out) if isinstance(out_shape, tuple) else vmem(1)[0], out_shape=out_shape, name=name,
        compiler_params=params(12), cost_estimate=pl.CostEstimate(flops=flops, bytes_accessed=moved, transcendentals=0),
    )(*args)


def scaled_cotangent(pack, gain):
    width = pack.shape[1]

    def body(pack_ref, g_ref, o_ref):
        o_ref[...] = (pack_ref[:TB].astype(F32) * g_ref[...]).T

    return small(body, "scaled_cotangent", 2, jax.ShapeDtypeStruct((width, TB), F32), pack, gain, flops=pack.size)


def partial_sums(x, scaled, copies):
    def body(x_ref, s_ref, o_ref):
        v = x_ref[...].reshape(scaled.shape).astype(F32)
        s = s_ref[...]
        sums = [jnp.sum(a, axis=0, keepdims=True) for a in (v, v * v, s, s * v)]
        block = jnp.concatenate([*sums, jnp.zeros((4, TB), F32)], axis=0)
        for i in range(copies):
            o_ref[i] = block

    return small(body, "partial_sums", 2, jax.ShapeDtypeStruct((copies, 8, TB), F32), x, scaled, flops=6 * x.size)


def statistics(sums):
    def body(s_ref, o_ref):
        total = s_ref[0]
        for i in range(1, sums.shape[0]):
            total += s_ref[i]
        mean = total[0:1] / D
        rstd = lax.rsqrt(total[1:2] / D - mean * mean + EPS)
        first = total[2:3] / D
        second = rstd * (total[3:4] / D - mean * first)
        o_ref[...] = jnp.concatenate([mean, rstd, first, second, jnp.zeros((4, TB), F32)], axis=0)

    return small(body, "statistics", 1, jax.ShapeDtypeStruct(sums.shape[1:], F32), sums)


def gradient(x, scaled, stats):
    def body(x_ref, s_ref, st_ref, o_ref):
        v = x_ref[...].reshape(scaled.shape).astype(F32)
        mean, rstd, first, second = (st_ref[i:i + 1] for i in range(4))
        xhat = (v - mean) * rstd
        o_ref[...] = (rstd * (s_ref[...] - first - xhat * second)).T.astype(BF16)

    return small(body, "gradient", 3, jax.ShapeDtypeStruct((TB, scaled.shape[0]), BF16), x, scaled, stats, flops=60000 * x.size)


def layer_norm(x, stats, gain, bias):
    width = gain.shape[1]

    def body(x_ref, st_ref, g_ref, b_ref, o_ref):
        v = x_ref[...].reshape(width, TB).astype(F32)
        xhat = (v - st_ref[0:1]) * st_ref[1:2]
        o_ref[...] = (xhat.T * g_ref[...] + b_ref[...]).astype(BF16)

    return small(body, "layer_norm", 4, jax.ShapeDtypeStruct((TB, width), BF16), x, stats, gain, bias, flops=4 * x.size)


def local(context, out_weight, residual, gain, bias, cot):
    m = lax.axis_index("mp").astype(jnp.int32)
    weights = out_weight[0][:, :, 0, :].transpose(1, 2, 0)
    weights = pltpu.with_memory_space_constraint(weights, pltpu.HBM)
    ctx = pltpu.with_memory_space_constraint(context[0], pltpu.HBM)

    far_sent, ctx, near_weights, own_weights = far_product(m.reshape(1), weights, ctx)
    far_got = swap_core(far_sent)
    far_top, far_low = far_sum(own_weights, ctx, far_got)
    near_got = swap_core(near_product(near_weights, ctx, far_top))
    relay_one = swap_y(far_top, 1)
    relay_three = swap_y(far_low, 3)
    one, three, keep_one, keep_three, mine = near_sum(own_weights, ctx, near_got, residual[0].T)
    direct_one = swap_y(one, 1)
    direct_three = swap_y(three, 3)
    on_one, on_three = relay_sum(keep_one, keep_three, relay_one, relay_three)
    sum_one = swap_y(on_one, 1)
    sum_three = swap_y(on_three, 3)
    mine, pack = add_direct(mine, direct_one, direct_three, cot[0], gain)
    pack_next = along_section(pack, -1)
    section_out = add_last(mine, sum_three, sum_one)
    got = lax.all_to_all(section_out, "dp", split_axis=0, concat_axis=0, tiled=True)
    got_next = along_section(got, 1)
    parts = pack_next[TB:TB + 3].astype(F32)
    scaled = scaled_cotangent(pack_next, parts[0:1] + parts[1:2] + parts[2:3])
    sums = lax.all_to_all(partial_sums(got, scaled, lax.axis_size("mp")), "mp", split_axis=0, concat_axis=0, tiled=True)
    stats = statistics(sums)
    stats_next = along_section(stats, 1)
    grad = gradient(got, scaled, stats)
    out = layer_norm(got_next, stats_next, gain, bias)
    return out[None], grad[None]


def solution(mesh):
    in_specs = (
        P("section", None, "mp"),
        P("section", "mp", None, "dp", None),
        P("section", None, ("mp", "dp")),
        P("section", "mp"),
        P("section", "mp"),
        P("section", "dp", "mp"),
    )
    out_specs = (P("section", "dp", "mp"), P("section", "dp", "mp"))
    return jax.shard_map(local, mesh=mesh, in_specs=in_specs, out_specs=out_specs, check_vma=False)
```

```python
import jax
import jax.numpy as jnp
from jax import lax
from jax.experimental import pallas as pl
from jax.experimental.pallas import tpu as pltpu
from jax.sharding import PartitionSpec as P

D = 12288
EPS = 1e-05
F32 = jnp.float32
BF16 = jnp.bfloat16
TB = 128
STEP = 2
ORDER = (2, 1, 3, 0)


def swap_core(x):
    n = lax.axis_size("mp")
    return lax.ppermute(x, "mp", [(i, i ^ 1) for i in range(n)])


def swap_y(x, pair):
    n = lax.axis_size("mp")
    return lax.ppermute(x, "mp", [(i, i ^ (2 * pair)) for i in range(n)])


def along_section(x, by):
    n = lax.axis_size("section")
    return lax.ppermute(x, "section", [(i, (i + by) % n) for i in range(n)])


def dot_t(w, c):
    return lax.dot_general(w, c, (((1,), (1,)), ((), ())), preferred_element_type=F32)


def params(mib):
    return pltpu.CompilerParams(vmem_limit_bytes=mib * 1024 * 1024)


def vmem(n):
    return [pl.BlockSpec(memory_space=pltpu.VMEM)] * n


def cost(n, rows, depth, toks):
    return pl.CostEstimate(flops=2 * n * rows * depth * toks, bytes_accessed=2 * n * rows * (depth + 2 * toks) + 2 * toks * depth, transcendentals=0)


def block_of(me, order, core):
    return (((me >> 1) ^ order) << 1) + core


def far_product(me, weights, ctx):
    rows, depth = weights.shape[1:]
    toks = ctx.shape[0]
    n_parts = 4

    def body(me_ref, w_ref, c_ref, far_ref, ctx_ref, far_w, c_sem, w_sem):
        me = me_ref[0]

        def c_copy(i):
            part = pl.ds(i * (toks // n_parts), toks // n_parts)
            return pltpu.make_async_copy(c_ref.at[part], ctx_ref.at[part], c_sem.at[i])

        w_copy = pltpu.make_async_copy(w_ref.at[block_of(me, ORDER[0], 1 - (me & 1))], far_w, w_sem)
        w_copy.start()
        for i in range(n_parts):
            c_copy(i).start()
        w_copy.wait()
        for i in range(n_parts):
            c_copy(i).wait()
        for i in range(toks // (STEP * TB)):
            acc = dot_t(far_w[...], ctx_ref[pl.ds(i * STEP * TB, STEP * TB)])
            for b in range(STEP):
                far_ref[STEP * i + b] = acc[:, b * TB:(b + 1) * TB].astype(BF16)

    return pl.pallas_call(
        body,
        in_specs=[pl.BlockSpec(memory_space=pltpu.SMEM), pl.BlockSpec(memory_space=pltpu.HBM), pl.BlockSpec(memory_space=pltpu.HBM)],
        out_specs=vmem(2),
        out_shape=(jax.ShapeDtypeStruct((toks // TB, rows, TB), BF16), jax.ShapeDtypeStruct((toks, depth), BF16)),
        scratch_shapes=[pltpu.VMEM((rows, depth), BF16), pltpu.SemaphoreType.DMA((n_parts,)), pltpu.SemaphoreType.DMA],
        compiler_params=params(16), cost_estimate=cost(1, rows, depth, toks), name="far_product",
    )(me, weights, ctx)


def own_far_product(me, weights, ctx):
    rows, depth = weights.shape[1:]
    toks = ctx.shape[0]

    def body(me_ref, w_ref, c_ref, far_ref, near_w_ref, own_w_ref, far_w, far_sem, near_sem, own_sem):
        me = me_ref[0]
        core = me & 1
        far_copy = pltpu.make_async_copy(w_ref.at[block_of(me, ORDER[0], core)], far_w, far_sem)
        copies = [pltpu.make_async_copy(w_ref.at[block_of(me, ORDER[k], 1 - core)], near_w_ref.at[pl.ds((k - 1) * rows, rows)], near_sem.at[k - 1]) for k in range(1, 4)]
        copies += [pltpu.make_async_copy(w_ref.at[block_of(me, ORDER[k], core)], own_w_ref.at[pl.ds((k - 1) * rows, rows)], own_sem.at[k - 1]) for k in range(1, 4)]
        far_copy.start()
        for copy in copies:
            copy.start()
        far_copy.wait()
        for i in range(toks // (STEP * TB)):
            acc = dot_t(far_w[...], c_ref[pl.ds(i * STEP * TB, STEP * TB)])
            for b in range(STEP):
                far_ref[STEP * i + b] = acc[:, b * TB:(b + 1) * TB]
        for copy in copies:
            copy.wait()

    return pl.pallas_call(
        body,
        in_specs=[pl.BlockSpec(memory_space=pltpu.SMEM), pl.BlockSpec(memory_space=pltpu.HBM), *vmem(1)],
        out_specs=vmem(3),
        out_shape=(jax.ShapeDtypeStruct((toks // TB, rows, TB), F32), jax.ShapeDtypeStruct((3 * rows, depth), BF16), jax.ShapeDtypeStruct((3 * rows, depth), BF16)),
        scratch_shapes=[pltpu.VMEM((rows, depth), BF16), pltpu.SemaphoreType.DMA, pltpu.SemaphoreType.DMA((3,)), pltpu.SemaphoreType.DMA((3,))],
        compiler_params=params(16), cost_estimate=cost(2, rows, depth, toks), name="own_far_product",
    )(me, weights, ctx)


def near_product(weights, ctx, after):
    toks, depth = ctx.shape
    rows = weights.shape[0] // 3

    def body(w_ref, c_ref, after_ref, o_ref):
        for i in range(toks // (STEP * TB)):
            acc = dot_t(w_ref[...], c_ref[pl.ds(i * STEP * TB, STEP * TB)])
            for b in range(STEP):
                for k in range(3):
                    o_ref[k, STEP * i + b] = acc[k * rows:(k + 1) * rows, b * TB:(b + 1) * TB].astype(BF16)

    return pl.pallas_call(
        body, in_specs=[*vmem(2), pl.BlockSpec(memory_space=pl.ANY)], out_specs=vmem(1)[0], out_shape=jax.ShapeDtypeStruct((3, toks // TB, rows, TB), BF16),
        compiler_params=params(16), cost_estimate=cost(3, rows, depth, toks), name="near_product",
    )(weights, ctx, after)


def far_sum(own, other):
    half = own.shape[1] // 2

    def body(own_ref, other_ref, top_ref, low_ref):
        top_ref[...] = (own_ref[:, :half] + other_ref[:, :half].astype(F32)).astype(BF16)
        low_ref[...] = (own_ref[:, half:] + other_ref[:, half:].astype(F32)).astype(BF16)

    shape = jax.ShapeDtypeStruct((own.shape[0], half, own.shape[2]), BF16)
    return pl.pallas_call(
        body, in_specs=vmem(2), out_specs=vmem(2), out_shape=(shape, shape), name="far_sum", compiler_params=params(8),
        cost_estimate=pl.CostEstimate(flops=own.size, bytes_accessed=8 * own.size, transcendentals=0),
    )(own, other)


def near_sum(weights, ctx, other, residual):
    toks, depth = ctx.shape
    rows = weights.shape[0] // 3
    half = rows // 2

    def body(w_ref, c_ref, r_ref, res_ref, one_ref, three_ref, keep_one_ref, keep_three_ref, mine_ref):
        for i in range(toks // (STEP * TB)):
            acc = dot_t(w_ref[...], c_ref[pl.ds(i * STEP * TB, STEP * TB)])
            for b in range(STEP):
                t = STEP * i + b
                cut = slice(b * TB, (b + 1) * TB)
                one = acc[:rows, cut] + r_ref[0, t].astype(F32)
                one_ref[t] = one[:half].astype(BF16)
                keep_one_ref[t] = one[half:]
                three = acc[rows:2 * rows, cut] + r_ref[1, t].astype(F32)
                three_ref[t] = three[half:].astype(BF16)
                keep_three_ref[t] = three[:half]
                mine_ref[t] = acc[2 * rows:, cut] + r_ref[2, t].astype(F32) + res_ref[:, t * TB:(t + 1) * TB].astype(F32)

    part = lambda dtype: jax.ShapeDtypeStruct((toks // TB, half, TB), dtype)
    return pl.pallas_call(
        body, in_specs=vmem(4), out_specs=vmem(5),
        out_shape=(part(BF16), part(BF16), part(F32), part(F32), jax.ShapeDtypeStruct((toks // TB, rows, TB), F32)),
        compiler_params=params(20), cost_estimate=cost(3, rows, depth, toks), name="near_sum",
    )(weights, ctx, other, residual)


def add_direct(mine, top, low, cot, gain):
    half = top.shape[1]
    width = cot.shape[1]

    def body(mine_ref, top_ref, low_ref, cot_ref, gain_ref, o_ref, pack_ref):
        pack_ref[:TB] = cot_ref[...]
        g = gain_ref[...]
        hi = g.astype(BF16)
        g = g - hi.astype(F32)
        mid = g.astype(BF16)
        low = (g - mid.astype(F32)).astype(BF16)
        row = lax.broadcasted_iota(jnp.int32, (16, width), 0)
        parts = jnp.where(row == 0, hi.astype(F32), jnp.where(row == 1, mid.astype(F32), jnp.where(row == 2, low.astype(F32), 0.0)))
        pack_ref[TB:] = parts.astype(BF16)
        o_ref[:, :half] = mine_ref[:, :half] + top_ref[...].astype(F32)
        o_ref[:, half:] = mine_ref[:, half:] + low_ref[...].astype(F32)

    return pl.pallas_call(
        body, in_specs=vmem(5), out_specs=vmem(2), out_shape=(jax.ShapeDtypeStruct(mine.shape, F32), jax.ShapeDtypeStruct((TB + 16, width), BF16)),
        name="add_direct", compiler_params=params(8),
        cost_estimate=pl.CostEstimate(flops=1 * mine.size, bytes_accessed=9 * mine.size, transcendentals=0),
    )(mine, top, low, cot, gain)


def add_last(mine, top, low):
    half = top.shape[1]

    def body(mine_ref, top_ref, low_ref, o_ref):
        o_ref[:, :half] = (mine_ref[:, :half] + top_ref[...].astype(F32)).astype(BF16)
        o_ref[:, half:] = (mine_ref[:, half:] + low_ref[...].astype(F32)).astype(BF16)

    return pl.pallas_call(
        body, in_specs=vmem(3), out_specs=vmem(1)[0], out_shape=jax.ShapeDtypeStruct(mine.shape, BF16), name="add_last", compiler_params=params(8),
        cost_estimate=pl.CostEstimate(flops=20000 * mine.size, bytes_accessed=7 * mine.size, transcendentals=0),
    )(mine, top, low)


def relay_sum(keep_one, keep_three, from_one, from_three):
    def body(keep_one_ref, keep_three_ref, from_one_ref, from_three_ref, one_ref, three_ref):
        one_ref[...] = (keep_one_ref[...] + from_three_ref[...].astype(F32)).astype(BF16)
        three_ref[...] = (keep_three_ref[...] + from_one_ref[...].astype(F32)).astype(BF16)

    shape = jax.ShapeDtypeStruct(keep_one.shape, BF16)
    return pl.pallas_call(
        body, in_specs=vmem(4), out_specs=vmem(2), out_shape=(shape, shape), name="relay_sum", compiler_params=params(8),
        cost_estimate=pl.CostEstimate(flops=2 * keep_one.size, bytes_accessed=16 * keep_one.size, transcendentals=0),
    )(keep_one, keep_three, from_one, from_three)


def small(body, name, n_in, out_shape, *args, flops=0):
    n_out = len(out_shape) if isinstance(out_shape, tuple) else 1
    moved = sum(a.size * a.dtype.itemsize for a in args)
    return pl.pallas_call(
        body, in_specs=vmem(n_in), out_specs=vmem(n_out) if isinstance(out_shape, tuple) else vmem(1)[0], out_shape=out_shape, name=name,
        compiler_params=params(12), cost_estimate=pl.CostEstimate(flops=flops, bytes_accessed=moved, transcendentals=0),
    )(*args)


def scaled_cotangent(pack, gain):
    width = pack.shape[1]

    def body(pack_ref, g_ref, o_ref):
        o_ref[...] = (pack_ref[:TB].astype(F32) * g_ref[...]).T

    return small(body, "scaled_cotangent", 2, jax.ShapeDtypeStruct((width, TB), F32), pack, gain, flops=pack.size)


def partial_sums(x, scaled, copies):
    def body(x_ref, s_ref, o_ref):
        groups, rows = x.shape[:2]
        totals = [jnp.zeros((rows, TB), F32)] * 4
        for i in range(groups):
            v = x_ref[i].astype(F32)
            s = s_ref[i * rows:(i + 1) * rows]
            totals = [t + a for t, a in zip(totals, (v, v * v, s, s * v))]
        sums = [jnp.sum(t, axis=0, keepdims=True) for t in totals]
        block = jnp.concatenate([*sums, jnp.zeros((4, TB), F32)], axis=0)
        for i in range(copies):
            o_ref[i] = block

    return small(body, "partial_sums", 2, jax.ShapeDtypeStruct((copies, 8, TB), F32), x, scaled, flops=6 * x.size)


def statistics(sums):
    def body(s_ref, o_ref):
        total = s_ref[0]
        for i in range(1, sums.shape[0]):
            total += s_ref[i]
        mean = total[0:1] / D
        rstd = lax.rsqrt(total[1:2] / D - mean * mean + EPS)
        first = total[2:3] / D
        second = rstd * (total[3:4] / D - mean * first)
        o_ref[...] = jnp.concatenate([mean, rstd, first, second, jnp.zeros((4, TB), F32)], axis=0)

    return small(body, "statistics", 1, jax.ShapeDtypeStruct(sums.shape[1:], F32), sums)


def gradient(x, scaled, stats):
    def body(x_ref, s_ref, st_ref, o_ref):
        v = x_ref[...].reshape(scaled.shape).astype(F32)
        mean, rstd, first, second = (st_ref[i:i + 1] for i in range(4))
        xhat = (v - mean) * rstd
        o_ref[...] = (rstd * (s_ref[...] - first - xhat * second)).T.astype(BF16)

    return small(body, "gradient", 3, jax.ShapeDtypeStruct((TB, scaled.shape[0]), BF16), x, scaled, stats, flops=60000 * x.size)


def layer_norm(x, stats, gain, bias):
    width = gain.shape[1]

    def body(x_ref, st_ref, g_ref, b_ref, o_ref):
        v = x_ref[...].reshape(width, TB).astype(F32)
        xhat = (v - st_ref[0:1]) * st_ref[1:2]
        o_ref[...] = (xhat.T * g_ref[...] + b_ref[...]).astype(BF16)

    return small(body, "layer_norm", 4, jax.ShapeDtypeStruct((TB, width), BF16), x, stats, gain, bias, flops=4 * x.size)


def local(context, out_weight, residual, gain, bias, cot):
    m = lax.axis_index("mp").astype(jnp.int32)
    weights = out_weight[0][:, :, 0, :].transpose(1, 2, 0)
    weights = pltpu.with_memory_space_constraint(weights, pltpu.HBM)
    ctx = pltpu.with_memory_space_constraint(context[0], pltpu.HBM)

    far_sent, ctx = far_product(m.reshape(1), weights, ctx)
    far_got = swap_core(far_sent)
    far_own, near_weights, own_weights = own_far_product(m.reshape(1), weights, ctx)
    far_top, far_low = far_sum(far_own, far_got)
    near_got = swap_core(near_product(near_weights, ctx, far_top))
    relay_one = swap_y(far_top, 1)
    relay_three = swap_y(far_low, 3)
    one, three, keep_one, keep_three, mine = near_sum(own_weights, ctx, near_got, residual[0].T)
    direct_one = swap_y(one, 1)
    direct_three = swap_y(three, 3)
    on_one, on_three = relay_sum(keep_one, keep_three, relay_one, relay_three)
    sum_one = swap_y(on_one, 1)
    sum_three = swap_y(on_three, 3)
    mine, pack = add_direct(mine, direct_one, direct_three, cot[0], gain)
    pack_next = along_section(pack, -1)
    section_out = add_last(mine, sum_three, sum_one)
    got = lax.all_to_all(section_out, "dp", split_axis=0, concat_axis=0, tiled=True)
    got_next = along_section(got, 1)
    parts = pack_next[TB:TB + 3].astype(F32)
    scaled = scaled_cotangent(pack_next, parts[0:1] + parts[1:2] + parts[2:3])
    sums = lax.all_to_all(partial_sums(got, scaled, lax.axis_size("mp")), "mp", split_axis=0, concat_axis=0, tiled=True)
    stats = statistics(sums)
    stats_next = along_section(stats, 1)
    grad = gradient(got, scaled, stats)
    out = layer_norm(got_next, stats_next, gain, bias)
    return out[None], grad[None]


def solution(mesh):
    in_specs = (
        P("section", None, "mp"),
        P("section", "mp", None, "dp", None),
        P("section", None, ("mp", "dp")),
        P("section", "mp"),
        P("section", "mp"),
        P("section", "dp", "mp"),
    )
    out_specs = (P("section", "dp", "mp"), P("section", "dp", "mp"))
    return jax.shard_map(local, mesh=mesh, in_specs=in_specs, out_specs=out_specs, check_vma=False)
```

```python
import jax
import jax.numpy as jnp
from jax import lax
from jax.experimental import pallas as pl
from jax.experimental.pallas import tpu as pltpu
from jax.sharding import PartitionSpec as P

D = 12288
EPS = 1e-05
F32 = jnp.float32
BF16 = jnp.bfloat16
TB = 128
STEP = 2
ORDER = (2, 1, 3, 0)


def swap_core(x):
    n = lax.axis_size("mp")
    return lax.ppermute(x, "mp", [(i, i ^ 1) for i in range(n)])


def swap_y(x, pair):
    n = lax.axis_size("mp")
    return lax.ppermute(x, "mp", [(i, i ^ (2 * pair)) for i in range(n)])


def along_section(x, by):
    n = lax.axis_size("section")
    return lax.ppermute(x, "section", [(i, (i + by) % n) for i in range(n)])


def dot_t(w, c):
    return lax.dot_general(w, c, (((1,), (1,)), ((), ())), preferred_element_type=F32)


def params(mib):
    return pltpu.CompilerParams(vmem_limit_bytes=mib * 1024 * 1024)


def vmem(n):
    return [pl.BlockSpec(memory_space=pltpu.VMEM)] * n


def cost(n, rows, depth, toks):
    return pl.CostEstimate(flops=2 * n * rows * depth * toks, bytes_accessed=2 * n * rows * (depth + 2 * toks) + 2 * toks * depth, transcendentals=0)


def block_of(me, order, core):
    return (((me >> 1) ^ order) << 1) + core


def sent_products(me, weights, ctx):
    rows, depth = weights.shape[1:]
    toks = ctx.shape[0]
    n_parts = 4

    def body(me_ref, w_ref, c_ref, sent_ref, ctx_ref, sent_w, c_sem, w_sem):
        me = me_ref[0]
        copies = [pltpu.make_async_copy(w_ref.at[block_of(me, ORDER[k], 1 - (me & 1))], sent_w.at[pl.ds(k * rows, rows)], w_sem.at[k]) for k in range(4)]
        for i in range(n_parts):
            part = pl.ds(i * (toks // n_parts), toks // n_parts)
            copies.append(pltpu.make_async_copy(c_ref.at[part], ctx_ref.at[part], c_sem.at[i]))
        for copy in copies:
            copy.start()
        for copy in copies:
            copy.wait()
        for i in range(toks // (STEP * TB)):
            acc = dot_t(sent_w[...], ctx_ref[pl.ds(i * STEP * TB, STEP * TB)])
            for b in range(STEP):
                for k in range(4):
                    sent_ref[k, STEP * i + b] = acc[k * rows:(k + 1) * rows, b * TB:(b + 1) * TB].astype(BF16)

    return pl.pallas_call(
        body,
        in_specs=[pl.BlockSpec(memory_space=pltpu.SMEM), pl.BlockSpec(memory_space=pltpu.HBM), pl.BlockSpec(memory_space=pltpu.HBM)],
        out_specs=vmem(2),
        out_shape=(jax.ShapeDtypeStruct((4, toks // TB, rows, TB), BF16), jax.ShapeDtypeStruct((toks, depth), BF16)),
        scratch_shapes=[pltpu.VMEM((4 * rows, depth), BF16), pltpu.SemaphoreType.DMA((n_parts,)), pltpu.SemaphoreType.DMA((4,))],
        compiler_params=params(16), cost_estimate=cost(4, rows, depth, toks), name="sent_products",
    )(me, weights, ctx)


def own_far_product(me, weights, ctx):
    rows, depth = weights.shape[1:]
    toks = ctx.shape[0]

    def body(me_ref, w_ref, c_ref, far_ref, own_w_ref, far_w, far_sem, own_sem):
        me = me_ref[0]
        core = me & 1
        far_copy = pltpu.make_async_copy(w_ref.at[block_of(me, ORDER[0], core)], far_w, far_sem)
        copies = [pltpu.make_async_copy(w_ref.at[block_of(me, ORDER[k], core)], own_w_ref.at[pl.ds((k - 1) * rows, rows)], own_sem.at[k - 1]) for k in range(1, 4)]
        far_copy.start()
        for copy in copies:
            copy.start()
        far_copy.wait()
        for i in range(toks // (STEP * TB)):
            acc = dot_t(far_w[...], c_ref[pl.ds(i * STEP * TB, STEP * TB)])
            for b in range(STEP):
                far_ref[STEP * i + b] = acc[:, b * TB:(b + 1) * TB]
        for copy in copies:
            copy.wait()

    return pl.pallas_call(
        body,
        in_specs=[pl.BlockSpec(memory_space=pltpu.SMEM), pl.BlockSpec(memory_space=pltpu.HBM), *vmem(1)],
        out_specs=vmem(2),
        out_shape=(jax.ShapeDtypeStruct((toks // TB, rows, TB), F32), jax.ShapeDtypeStruct((3 * rows, depth), BF16)),
        scratch_shapes=[pltpu.VMEM((rows, depth), BF16), pltpu.SemaphoreType.DMA, pltpu.SemaphoreType.DMA((3,))],
        compiler_params=params(16), cost_estimate=cost(2, rows, depth, toks), name="own_far_product",
    )(me, weights, ctx)


def far_sum(own, other):
    half = own.shape[1] // 2

    def body(own_ref, other_ref, top_ref, low_ref):
        top_ref[...] = (own_ref[:, :half] + other_ref[0, :, :half].astype(F32)).astype(BF16)
        low_ref[...] = (own_ref[:, half:] + other_ref[0, :, half:].astype(F32)).astype(BF16)

    shape = jax.ShapeDtypeStruct((own.shape[0], half, own.shape[2]), BF16)
    return pl.pallas_call(
        body, in_specs=vmem(2), out_specs=vmem(2), out_shape=(shape, shape), name="far_sum", compiler_params=params(8),
        cost_estimate=pl.CostEstimate(flops=own.size, bytes_accessed=8 * own.size, transcendentals=0),
    )(own, other)


def near_sum(weights, ctx, other, residual):
    toks, depth = ctx.shape
    rows = weights.shape[0] // 3
    half = rows // 2

    def body(w_ref, c_ref, r_ref, res_ref, one_ref, three_ref, keep_one_ref, keep_three_ref, mine_ref):
        for i in range(toks // (STEP * TB)):
            acc = dot_t(w_ref[...], c_ref[pl.ds(i * STEP * TB, STEP * TB)])
            for b in range(STEP):
                t = STEP * i + b
                cut = slice(b * TB, (b + 1) * TB)
                one = acc[:rows, cut] + r_ref[1, t].astype(F32)
                one_ref[t] = one[:half].astype(BF16)
                keep_one_ref[t] = one[half:]
                three = acc[rows:2 * rows, cut] + r_ref[2, t].astype(F32)
                three_ref[t] = three[half:].astype(BF16)
                keep_three_ref[t] = three[:half]
                mine_ref[t] = acc[2 * rows:, cut] + r_ref[3, t].astype(F32) + res_ref[:, t * TB:(t + 1) * TB].astype(F32)

    part = lambda dtype: jax.ShapeDtypeStruct((toks // TB, half, TB), dtype)
    return pl.pallas_call(
        body, in_specs=vmem(4), out_specs=vmem(5),
        out_shape=(part(BF16), part(BF16), part(F32), part(F32), jax.ShapeDtypeStruct((toks // TB, rows, TB), F32)),
        compiler_params=params(20), cost_estimate=cost(3, rows, depth, toks), name="near_sum",
    )(weights, ctx, other, residual)


def add_direct(mine, top, low, cot, gain):
    half = top.shape[1]
    width = cot.shape[1]

    def body(mine_ref, top_ref, low_ref, cot_ref, gain_ref, o_ref, pack_ref):
        pack_ref[:TB] = cot_ref[...]
        g = gain_ref[...]
        hi = g.astype(BF16)
        g = g - hi.astype(F32)
        mid = g.astype(BF16)
        low = (g - mid.astype(F32)).astype(BF16)
        row = lax.broadcasted_iota(jnp.int32, (16, width), 0)
        parts = jnp.where(row == 0, hi.astype(F32), jnp.where(row == 1, mid.astype(F32), jnp.where(row == 2, low.astype(F32), 0.0)))
        pack_ref[TB:] = parts.astype(BF16)
        o_ref[:, :half] = mine_ref[:, :half] + top_ref[...].astype(F32)
        o_ref[:, half:] = mine_ref[:, half:] + low_ref[...].astype(F32)

    return pl.pallas_call(
        body, in_specs=vmem(5), out_specs=vmem(2), out_shape=(jax.ShapeDtypeStruct(mine.shape, F32), jax.ShapeDtypeStruct((TB + 16, width), BF16)),
        name="add_direct", compiler_params=params(8),
        cost_estimate=pl.CostEstimate(flops=1 * mine.size, bytes_accessed=9 * mine.size, transcendentals=0),
    )(mine, top, low, cot, gain)


def add_last(mine, top, low):
    half = top.shape[1]

    def body(mine_ref, top_ref, low_ref, o_ref):
        o_ref[:, :half] = (mine_ref[:, :half] + top_ref[...].astype(F32)).astype(BF16)
        o_ref[:, half:] = (mine_ref[:, half:] + low_ref[...].astype(F32)).astype(BF16)

    return pl.pallas_call(
        body, in_specs=vmem(3), out_specs=vmem(1)[0], out_shape=jax.ShapeDtypeStruct(mine.shape, BF16), name="add_last", compiler_params=params(8),
        cost_estimate=pl.CostEstimate(flops=20000 * mine.size, bytes_accessed=7 * mine.size, transcendentals=0),
    )(mine, top, low)


def relay_sum(keep_one, keep_three, from_one, from_three):
    def body(keep_one_ref, keep_three_ref, from_one_ref, from_three_ref, one_ref, three_ref):
        one_ref[...] = (keep_one_ref[...] + from_three_ref[...].astype(F32)).astype(BF16)
        three_ref[...] = (keep_three_ref[...] + from_one_ref[...].astype(F32)).astype(BF16)

    shape = jax.ShapeDtypeStruct(keep_one.shape, BF16)
    return pl.pallas_call(
        body, in_specs=vmem(4), out_specs=vmem(2), out_shape=(shape, shape), name="relay_sum", compiler_params=params(8),
        cost_estimate=pl.CostEstimate(flops=2 * keep_one.size, bytes_accessed=16 * keep_one.size, transcendentals=0),
    )(keep_one, keep_three, from_one, from_three)


def small(body, name, n_in, out_shape, *args, flops=0):
    n_out = len(out_shape) if isinstance(out_shape, tuple) else 1
    moved = sum(a.size * a.dtype.itemsize for a in args)
    return pl.pallas_call(
        body, in_specs=vmem(n_in), out_specs=vmem(n_out) if isinstance(out_shape, tuple) else vmem(1)[0], out_shape=out_shape, name=name,
        compiler_params=params(12), cost_estimate=pl.CostEstimate(flops=flops, bytes_accessed=moved, transcendentals=0),
    )(*args)


def scaled_cotangent(pack, gain):
    width = pack.shape[1]

    def body(pack_ref, g_ref, o_ref):
        o_ref[...] = (pack_ref[:TB].astype(F32) * g_ref[...]).T

    return small(body, "scaled_cotangent", 2, jax.ShapeDtypeStruct((width, TB), F32), pack, gain, flops=pack.size)


def partial_sums(x, scaled, copies):
    def body(x_ref, s_ref, o_ref):
        groups, rows = x.shape[:2]
        totals = [jnp.zeros((rows, TB), F32)] * 4
        for i in range(groups):
            v = x_ref[i].astype(F32)
            s = s_ref[i * rows:(i + 1) * rows]
            totals = [t + a for t, a in zip(totals, (v, v * v, s, s * v))]
        sums = [jnp.sum(t, axis=0, keepdims=True) for t in totals]
        block = jnp.concatenate([*sums, jnp.zeros((4, TB), F32)], axis=0)
        for i in range(copies):
            o_ref[i] = block

    return small(body, "partial_sums", 2, jax.ShapeDtypeStruct((copies, 8, TB), F32), x, scaled, flops=6 * x.size)


def statistics(sums):
    def body(s_ref, o_ref):
        total = s_ref[0]
        for i in range(1, sums.shape[0]):
            total += s_ref[i]
        mean = total[0:1] / D
        rstd = lax.rsqrt(total[1:2] / D - mean * mean + EPS)
        first = total[2:3] / D
        second = rstd * (total[3:4] / D - mean * first)
        o_ref[...] = jnp.concatenate([mean, rstd, first, second, jnp.zeros((4, TB), F32)], axis=0)

    return small(body, "statistics", 1, jax.ShapeDtypeStruct(sums.shape[1:], F32), sums)


def gradient(x, scaled, stats):
    def body(x_ref, s_ref, st_ref, o_ref):
        v = x_ref[...].reshape(scaled.shape).astype(F32)
        mean, rstd, first, second = (st_ref[i:i + 1] for i in range(4))
        xhat = (v - mean) * rstd
        o_ref[...] = (rstd * (s_ref[...] - first - xhat * second)).T.astype(BF16)

    return small(body, "gradient", 3, jax.ShapeDtypeStruct((TB, scaled.shape[0]), BF16), x, scaled, stats, flops=60000 * x.size)


def layer_norm(x, stats, gain, bias):
    width = gain.shape[1]

    def body(x_ref, st_ref, g_ref, b_ref, o_ref):
        v = x_ref[...].reshape(width, TB).astype(F32)
        xhat = (v - st_ref[0:1]) * st_ref[1:2]
        o_ref[...] = (xhat.T * g_ref[...] + b_ref[...]).astype(BF16)

    return small(body, "layer_norm", 4, jax.ShapeDtypeStruct((TB, width), BF16), x, stats, gain, bias, flops=4 * x.size)


def local(context, out_weight, residual, gain, bias, cot):
    m = lax.axis_index("mp").astype(jnp.int32)
    weights = out_weight[0][:, :, 0, :].transpose(1, 2, 0)
    weights = pltpu.with_memory_space_constraint(weights, pltpu.HBM)
    ctx = pltpu.with_memory_space_constraint(context[0], pltpu.HBM)

    sent, ctx = sent_products(m.reshape(1), weights, ctx)
    got = swap_core(sent)
    far_own, own_weights = own_far_product(m.reshape(1), weights, ctx)
    far_top, far_low = far_sum(far_own, got)
    relay_one = swap_y(far_top, 1)
    relay_three = swap_y(far_low, 3)
    one, three, keep_one, keep_three, mine = near_sum(own_weights, ctx, got, residual[0].T)
    direct_one = swap_y(one, 1)
    direct_three = swap_y(three, 3)
    on_one, on_three = relay_sum(keep_one, keep_three, relay_one, relay_three)
    sum_one = swap_y(on_one, 1)
    sum_three = swap_y(on_three, 3)
    mine, pack = add_direct(mine, direct_one, direct_three, cot[0], gain)
    pack_next = along_section(pack, -1)
    section_out = add_last(mine, sum_three, sum_one)
    got = lax.all_to_all(section_out, "dp", split_axis=0, concat_axis=0, tiled=True)
    got_next = along_section(got, 1)
    parts = pack_next[TB:TB + 3].astype(F32)
    scaled = scaled_cotangent(pack_next, parts[0:1] + parts[1:2] + parts[2:3])
    sums = lax.all_to_all(partial_sums(got, scaled, lax.axis_size("mp")), "mp", split_axis=0, concat_axis=0, tiled=True)
    stats = statistics(sums)
    stats_next = along_section(stats, 1)
    grad = gradient(got, scaled, stats)
    out = layer_norm(got_next, stats_next, gain, bias)
    return out[None], grad[None]


def solution(mesh):
    in_specs = (
        P("section", None, "mp"),
        P("section", "mp", None, "dp", None),
        P("section", None, ("mp", "dp")),
        P("section", "mp"),
        P("section", "mp"),
        P("section", "dp", "mp"),
    )
    out_specs = (P("section", "dp", "mp"), P("section", "dp", "mp"))
    return jax.shard_map(local, mesh=mesh, in_specs=in_specs, out_specs=out_specs, check_vma=False)
```

```python
import jax
import jax.numpy as jnp
from jax import lax
from jax.experimental import pallas as pl
from jax.experimental.pallas import tpu as pltpu
from jax.sharding import PartitionSpec as P

D = 12288
EPS = 1e-05
F32 = jnp.float32
BF16 = jnp.bfloat16
TB = 128
STEP = 2
ORDER = (2, 1, 3, 0)


def swap_core(x):
    n = lax.axis_size("mp")
    return lax.ppermute(x, "mp", [(i, i ^ 1) for i in range(n)])


def swap_y(x, pair):
    n = lax.axis_size("mp")
    return lax.ppermute(x, "mp", [(i, i ^ (2 * pair)) for i in range(n)])


def along_section(x, by):
    n = lax.axis_size("section")
    return lax.ppermute(x, "section", [(i, (i + by) % n) for i in range(n)])


def dot_t(w, c):
    return lax.dot_general(w, c, (((1,), (1,)), ((), ())), preferred_element_type=F32)


def params(mib):
    return pltpu.CompilerParams(vmem_limit_bytes=mib * 1024 * 1024)


def vmem(n):
    return [pl.BlockSpec(memory_space=pltpu.VMEM)] * n


def cost(n, rows, depth, toks):
    return pl.CostEstimate(flops=2 * n * rows * depth * toks, bytes_accessed=2 * n * rows * (depth + 2 * toks) + 2 * toks * depth, transcendentals=0)


def block_of(me, order, core):
    return (((me >> 1) ^ order) << 1) + core


def sent_products(me, weights, ctx):
    rows, depth = weights.shape[1:]
    toks = ctx.shape[0]
    n_parts = 4

    def body(me_ref, w_ref, c_ref, sent_ref, ctx_ref, sent_w, c_sem, w_sem):
        me = me_ref[0]
        copies = [pltpu.make_async_copy(w_ref.at[block_of(me, ORDER[k], 1 - (me & 1))], sent_w.at[pl.ds(k * rows, rows)], w_sem.at[k]) for k in range(4)]
        for i in range(n_parts):
            part = pl.ds(i * (toks // n_parts), toks // n_parts)
            copies.append(pltpu.make_async_copy(c_ref.at[part], ctx_ref.at[part], c_sem.at[i]))
        for copy in copies:
            copy.start()
        for copy in copies:
            copy.wait()
        for i in range(toks // (STEP * TB)):
            acc = dot_t(sent_w[...], ctx_ref[pl.ds(i * STEP * TB, STEP * TB)])
            for b in range(STEP):
                for k in range(4):
                    sent_ref[k, STEP * i + b] = acc[k * rows:(k + 1) * rows, b * TB:(b + 1) * TB].astype(BF16)

    return pl.pallas_call(
        body,
        in_specs=[pl.BlockSpec(memory_space=pltpu.SMEM), pl.BlockSpec(memory_space=pltpu.HBM), pl.BlockSpec(memory_space=pltpu.HBM)],
        out_specs=vmem(2),
        out_shape=(jax.ShapeDtypeStruct((4, toks // TB, rows, TB), BF16), jax.ShapeDtypeStruct((toks, depth), BF16)),
        scratch_shapes=[pltpu.VMEM((4 * rows, depth), BF16), pltpu.SemaphoreType.DMA((n_parts,)), pltpu.SemaphoreType.DMA((4,))],
        compiler_params=params(16), cost_estimate=cost(4, rows, depth, toks), name="sent_products",
    )(me, weights, ctx)


def own_far_product(me, weights, ctx):
    rows, depth = weights.shape[1:]
    toks = ctx.shape[0]

    def body(me_ref, w_ref, c_ref, far_ref, own_w_ref, far_w, far_sem, own_sem):
        me = me_ref[0]
        core = me & 1
        far_copy = pltpu.make_async_copy(w_ref.at[block_of(me, ORDER[0], core)], far_w, far_sem)
        copies = [pltpu.make_async_copy(w_ref.at[block_of(me, ORDER[k], core)], own_w_ref.at[pl.ds((k - 1) * rows, rows)], own_sem.at[k - 1]) for k in range(1, 4)]
        far_copy.start()
        for copy in copies:
            copy.start()
        far_copy.wait()
        for i in range(toks // (STEP * TB)):
            acc = dot_t(far_w[...], c_ref[pl.ds(i * STEP * TB, STEP * TB)])
            for b in range(STEP):
                far_ref[STEP * i + b] = acc[:, b * TB:(b + 1) * TB]
        for copy in copies:
            copy.wait()

    return pl.pallas_call(
        body,
        in_specs=[pl.BlockSpec(memory_space=pltpu.SMEM), pl.BlockSpec(memory_space=pltpu.HBM), *vmem(1)],
        out_specs=vmem(2),
        out_shape=(jax.ShapeDtypeStruct((toks // TB, rows, TB), F32), jax.ShapeDtypeStruct((3 * rows, depth), BF16)),
        scratch_shapes=[pltpu.VMEM((rows, depth), BF16), pltpu.SemaphoreType.DMA, pltpu.SemaphoreType.DMA((3,))],
        compiler_params=params(16), cost_estimate=cost(2, rows, depth, toks), name="own_far_product",
    )(me, weights, ctx)


def far_sum(own, other):
    half = own.shape[1] // 2

    def body(own_ref, other_ref, top_ref, low_ref):
        top_ref[...] = (own_ref[:, :half] + other_ref[0, :, :half].astype(F32)).astype(BF16)
        low_ref[...] = (own_ref[:, half:] + other_ref[0, :, half:].astype(F32)).astype(BF16)

    shape = jax.ShapeDtypeStruct((own.shape[0], half, own.shape[2]), BF16)
    return pl.pallas_call(
        body, in_specs=vmem(2), out_specs=vmem(2), out_shape=(shape, shape), name="far_sum", compiler_params=params(8),
        cost_estimate=pl.CostEstimate(flops=own.size, bytes_accessed=8 * own.size, transcendentals=0),
    )(own, other)


def near_sum(weights, ctx, other, residual):
    toks, depth = ctx.shape
    rows = weights.shape[0] // 3
    half = rows // 2

    def body(w_ref, c_ref, r_ref, res_ref, one_ref, three_ref, keep_one_ref, keep_three_ref, mine_ref):
        for i in range(toks // (STEP * TB)):
            acc = dot_t(w_ref[...], c_ref[pl.ds(i * STEP * TB, STEP * TB)])
            for b in range(STEP):
                t = STEP * i + b
                cut = slice(b * TB, (b + 1) * TB)
                one = acc[:rows, cut] + r_ref[1, t].astype(F32)
                one_ref[t] = one[:half].astype(BF16)
                keep_one_ref[t] = one[half:]
                three = acc[rows:2 * rows, cut] + r_ref[2, t].astype(F32)
                three_ref[t] = three[half:].astype(BF16)
                keep_three_ref[t] = three[:half]
                mine_ref[t] = acc[2 * rows:, cut] + r_ref[3, t].astype(F32) + res_ref[:, t * TB:(t + 1) * TB].astype(F32)

    part = lambda dtype: jax.ShapeDtypeStruct((toks // TB, half, TB), dtype)
    return pl.pallas_call(
        body, in_specs=vmem(4), out_specs=vmem(5),
        out_shape=(part(BF16), part(BF16), part(F32), part(F32), jax.ShapeDtypeStruct((toks // TB, rows, TB), F32)),
        compiler_params=params(20), cost_estimate=cost(3, rows, depth, toks), name="near_sum",
    )(weights, ctx, other, residual)


def add_direct(mine, top, low, cot, gain):
    half = top.shape[1]
    width = cot.shape[1]

    def body(mine_ref, top_ref, low_ref, cot_ref, gain_ref, o_ref, pack_ref):
        pack_ref[:TB] = cot_ref[...]
        g = gain_ref[...]
        hi = g.astype(BF16)
        g = g - hi.astype(F32)
        mid = g.astype(BF16)
        low = (g - mid.astype(F32)).astype(BF16)
        row = lax.broadcasted_iota(jnp.int32, (16, width), 0)
        parts = jnp.where(row == 0, hi.astype(F32), jnp.where(row == 1, mid.astype(F32), jnp.where(row == 2, low.astype(F32), 0.0)))
        pack_ref[TB:] = parts.astype(BF16)
        o_ref[:, :half] = mine_ref[:, :half] + top_ref[...].astype(F32)
        o_ref[:, half:] = mine_ref[:, half:] + low_ref[...].astype(F32)

    return pl.pallas_call(
        body, in_specs=vmem(5), out_specs=vmem(2), out_shape=(jax.ShapeDtypeStruct(mine.shape, F32), jax.ShapeDtypeStruct((TB + 16, width), BF16)),
        name="add_direct", compiler_params=params(8),
        cost_estimate=pl.CostEstimate(flops=1 * mine.size, bytes_accessed=9 * mine.size, transcendentals=0),
    )(mine, top, low, cot, gain)


def add_last(mine, top, low):
    half = top.shape[1]

    def body(mine_ref, top_ref, low_ref, o_ref):
        o_ref[:, :half] = (mine_ref[:, :half] + top_ref[...].astype(F32)).astype(BF16)
        o_ref[:, half:] = (mine_ref[:, half:] + low_ref[...].astype(F32)).astype(BF16)

    return pl.pallas_call(
        body, in_specs=vmem(3), out_specs=vmem(1)[0], out_shape=jax.ShapeDtypeStruct(mine.shape, BF16), name="add_last", compiler_params=params(8),
        cost_estimate=pl.CostEstimate(flops=20000 * mine.size, bytes_accessed=7 * mine.size, transcendentals=0),
    )(mine, top, low)


def relay_sum(keep_one, keep_three, from_one, from_three):
    def body(keep_one_ref, keep_three_ref, from_one_ref, from_three_ref, one_ref, three_ref):
        one_ref[...] = (keep_one_ref[...] + from_three_ref[...].astype(F32)).astype(BF16)
        three_ref[...] = (keep_three_ref[...] + from_one_ref[...].astype(F32)).astype(BF16)

    shape = jax.ShapeDtypeStruct(keep_one.shape, BF16)
    return pl.pallas_call(
        body, in_specs=vmem(4), out_specs=vmem(2), out_shape=(shape, shape), name="relay_sum", compiler_params=params(8),
        cost_estimate=pl.CostEstimate(flops=2 * keep_one.size, bytes_accessed=16 * keep_one.size, transcendentals=0),
    )(keep_one, keep_three, from_one, from_three)


def small(body, name, n_in, out_shape, *args, flops=0):
    n_out = len(out_shape) if isinstance(out_shape, tuple) else 1
    moved = sum(a.size * a.dtype.itemsize for a in args)
    return pl.pallas_call(
        body, in_specs=vmem(n_in), out_specs=vmem(n_out) if isinstance(out_shape, tuple) else vmem(1)[0], out_shape=out_shape, name=name,
        compiler_params=params(12), cost_estimate=pl.CostEstimate(flops=flops, bytes_accessed=moved, transcendentals=0),
    )(*args)


def scaled_cotangent(pack, gain):
    width = pack.shape[1]

    def body(pack_ref, g_ref, o_ref):
        o_ref[...] = (pack_ref[:TB].astype(F32) * g_ref[...]).T

    return small(body, "scaled_cotangent", 2, jax.ShapeDtypeStruct((width, TB), F32), pack, gain, flops=pack.size)


def partial_sums(x, scaled, copies):
    def body(x_ref, s_ref, o_ref):
        groups, rows = x.shape[:2]
        part = 48
        sums = [jnp.zeros((8, TB), F32)] * 4
        for r in range(0, rows, part):
            totals = [jnp.zeros((part, TB), F32)] * 4
            for i in range(groups):
                v = x_ref[i, r:r + part].astype(F32)
                s = s_ref[i * rows + r:i * rows + r + part]
                totals = [t + a for t, a in zip(totals, (v, v * v, s, s * v))]
            sums = [a + jnp.sum(t.reshape(part // 8, 8, TB), axis=0) for a, t in zip(sums, totals)]
        sums = [jnp.sum(a, axis=0, keepdims=True) for a in sums]
        block = jnp.concatenate([*sums, jnp.zeros((4, TB), F32)], axis=0)
        for i in range(copies):
            o_ref[i] = block

    return small(body, "partial_sums", 2, jax.ShapeDtypeStruct((copies, 8, TB), F32), x, scaled, flops=6 * x.size)


def statistics(sums):
    def body(s_ref, o_ref):
        total = s_ref[0]
        for i in range(1, sums.shape[0]):
            total += s_ref[i]
        mean = total[0:1] / D
        rstd = lax.rsqrt(total[1:2] / D - mean * mean + EPS)
        first = total[2:3] / D
        second = rstd * (total[3:4] / D - mean * first)
        o_ref[...] = jnp.concatenate([mean, rstd, first, second, jnp.zeros((4, TB), F32)], axis=0)

    return small(body, "statistics", 1, jax.ShapeDtypeStruct(sums.shape[1:], F32), sums)


def gradient(x, scaled, stats):
    def body(x_ref, s_ref, st_ref, o_ref):
        v = x_ref[...].reshape(scaled.shape).astype(F32)
        mean, rstd, first, second = (st_ref[i:i + 1] for i in range(4))
        xhat = (v - mean) * rstd
        o_ref[...] = (rstd * (s_ref[...] - first - xhat * second)).T.astype(BF16)

    return small(body, "gradient", 3, jax.ShapeDtypeStruct((TB, scaled.shape[0]), BF16), x, scaled, stats, flops=60000 * x.size)


def layer_norm(x, stats, gain, bias):
    width = gain.shape[1]

    def body(x_ref, st_ref, g_ref, b_ref, o_ref):
        v = x_ref[...].reshape(width, TB).astype(F32)
        xhat = (v - st_ref[0:1]) * st_ref[1:2]
        o_ref[...] = (xhat.T * g_ref[...] + b_ref[...]).astype(BF16)

    return small(body, "layer_norm", 4, jax.ShapeDtypeStruct((TB, width), BF16), x, stats, gain, bias, flops=4 * x.size)


def local(context, out_weight, residual, gain, bias, cot):
    m = lax.axis_index("mp").astype(jnp.int32)
    weights = out_weight[0][:, :, 0, :].transpose(1, 2, 0)
    weights = pltpu.with_memory_space_constraint(weights, pltpu.HBM)
    ctx = pltpu.with_memory_space_constraint(context[0], pltpu.HBM)

    sent, ctx = sent_products(m.reshape(1), weights, ctx)
    got = swap_core(sent)
    far_own, own_weights = own_far_product(m.reshape(1), weights, ctx)
    far_top, far_low = far_sum(far_own, got)
    relay_one = swap_y(far_top, 1)
    relay_three = swap_y(far_low, 3)
    one, three, keep_one, keep_three, mine = near_sum(own_weights, ctx, got, residual[0].T)
    direct_one = swap_y(one, 1)
    direct_three = swap_y(three, 3)
    on_one, on_three = relay_sum(keep_one, keep_three, relay_one, relay_three)
    sum_one = swap_y(on_one, 1)
    sum_three = swap_y(on_three, 3)
    mine, pack = add_direct(mine, direct_one, direct_three, cot[0], gain)
    pack_next = along_section(pack, -1)
    section_out = add_last(mine, sum_three, sum_one)
    got = lax.all_to_all(section_out, "dp", split_axis=0, concat_axis=0, tiled=True)
    got_next = along_section(got, 1)
    parts = pack_next[TB:TB + 3].astype(F32)
    scaled = scaled_cotangent(pack_next, parts[0:1] + parts[1:2] + parts[2:3])
    sums = lax.all_to_all(partial_sums(got, scaled, lax.axis_size("mp")), "mp", split_axis=0, concat_axis=0, tiled=True)
    stats = statistics(sums)
    stats_next = along_section(stats, 1)
    grad = gradient(got, scaled, stats)
    out = layer_norm(got_next, stats_next, gain, bias)
    return out[None], grad[None]


def solution(mesh):
    in_specs = (
        P("section", None, "mp"),
        P("section", "mp", None, "dp", None),
        P("section", None, ("mp", "dp")),
        P("section", "mp"),
        P("section", "mp"),
        P("section", "dp", "mp"),
    )
    out_specs = (P("section", "dp", "mp"), P("section", "dp", "mp"))
    return jax.shard_map(local, mesh=mesh, in_specs=in_specs, out_specs=out_specs, check_vma=False)
```
